256 devices in a mesh: frow: 16 (over z_hi, y), fcol: 16 (over z_lo, x, core).
Axes of the slice: x: 4, y: 4, z: 8 (z_hi: 4, z_lo: 2; z = z_hi * 2 + z_lo), core: 2. Of those that a mesh axis runs over, the one named last changes fastest.
Arguments:
- image: bfloat16 [2, 8192, 8192], P(None, 'frow', 'fcol'), may hold values from -6 to 6
- window_rows: float32 [8192], P('frow'), may hold values from 0.1 to 1.9
- window_cols: float32 [8192], P('fcol'), may hold values from 0.1 to 1.9
- w_terms: float32 [2], replicated, may hold values from 20 to 200
- facet_row_offset: int32 [16], replicated, may hold values from 0 to 65535
- facet_col_offset: int32 [16], replicated, may hold values from 0 to 65535
- band_offset: int32 [2], replicated, may hold values from 0 to 65535
- sub_row_offset: int32 [2], replicated, may hold values from 0 to 65535
- sub_column: int32 [2], replicated, may hold values from 0 to 1, as said below
Outputs:
- subgrids: float32 [2, 2, 512, 512], P(None, None, 'frow', 'fcol')
The draws below stay inside these ranges and needn't reach their ends.
Inputs may be any that keep to these rules, and one draw needn't show every extreme that they name: `sub_column`: every subgrid column holds exactly 1 subgrids.
All inputs are finite; a program needn't handle non-finite values.
Results may differ from the reference program's by a relative error of at most 0.0052.
Values sent between devices are 32-bit elements; how exact they have to be, the bound alone decides.
No kernel may reach another device: no remote copies, remote signals or barrier semaphores. Data moves between devices by JAX's collectives and lax.ppermute only.
A program may use at most 64 MiB of HBM per device.

```python
import math
import jax
import jax.numpy as jnp
from jax import lax

F = 512
SG = 512
IMAGE = 65536
COLS = 2
SUB = 2
NX = 8192
NY = 8192
N_FROW = 16
N_FCOL = 16


def draw_sub_column(key, part):
    order = jax.random.permutation(jax.random.fold_in(key, 17), SUB)
    return (order % COLS).astype(jnp.int32)


def plant(result, stream_key, low, high):
    longest = result.shape.index(max(result.shape))
    spots = []
    for shift in (0, 1):
        where = [jax.random.randint(jax.random.fold_in(stream_key, axis), (), 0, length) for axis, length in enumerate(result.shape)]
        where[longest] = (where[longest] + shift) % result.shape[longest]
        spots.append(tuple(where))
    return result.at[spots[0]].set(low).at[spots[1]].set(high)


def level_of(stream_key, shape, shards, low, high):
    def one(axis_at, blocks):
        draws = jax.random.uniform(jax.random.fold_in(jax.random.fold_in(stream_key, 6), axis_at), (blocks,), jnp.float32, low / len(shards), high / len(shards))
        return jnp.repeat(jnp.exp(draws), shape[axis_at] // blocks).reshape((-1,) + (1,) * (len(shape) - axis_at - 1))

    gain = one(*shards[0])
    for cut in shards[1:]:
        gain = gain * one(*cut)
    return gain


def gaussian(key, shape, width, limit, split=(), kind=jnp.bfloat16):
    level = level_of(key, shape, split, -0.22, 0.18) if split else 1.0
    result = jax.random.normal(key, shape, jnp.float32) * width * level
    return jnp.minimum(jnp.maximum(result, -limit), limit).astype(kind)


def setup_inputs(seed: int = 0) -> dict:
    arg_keys = jax.random.split(jax.random.key(seed), 10)
    return {
        "image": gaussian(arg_keys[0], (2, NX, NY), 1.0, 6.0, ((1, 16), (2, 16))),
        "window_rows": jnp.clip(1.0 + 0.18 * jax.random.normal(arg_keys[1], (NX,), jnp.float32), 0.1, 1.9),
        "window_cols": jnp.clip(1.0 + 0.18 * jax.random.normal(arg_keys[2], (NY,), jnp.float32), 0.1, 1.9),
        "w_terms": jnp.clip(jax.random.uniform(arg_keys[3], (COLS,), jnp.float32, 20.0, 200.0), 20.0, 200.0),
        "facet_row_offset": plant(jax.random.randint(arg_keys[4], (N_FROW,), 0, IMAGE), jax.random.fold_in(arg_keys[4], 1), 0, IMAGE - 1).astype(jnp.int32),
        "facet_col_offset": plant(jax.random.randint(arg_keys[5], (N_FCOL,), 0, IMAGE), jax.random.fold_in(arg_keys[5], 1), 0, IMAGE - 1).astype(jnp.int32),
        "band_offset": jax.random.randint(arg_keys[6], (COLS,), 0, IMAGE).astype(jnp.int32),
        "sub_row_offset": jax.random.randint(arg_keys[7], (SUB,), 0, IMAGE).astype(jnp.int32),
        "sub_column": draw_sub_column(jax.random.fold_in(arg_keys[9], 71), 0),
    }


def phase_index(first, second):
    high = first * (second // 256) % 256 * 256
    return (high + first * (second % 256)) % 65536

def dft_table(coords, freqs):
    angle = phase_index(coords, freqs).astype(jnp.float32) * (2.0 * math.pi / IMAGE)
    return (jnp.cos(angle).astype(jnp.bfloat16), (-jnp.sin(angle)).astype(jnp.bfloat16))

def coord_unit(coords):
    return (coords % IMAGE).astype(jnp.float32) / IMAGE - 0.5

def prepare(real_part, imag_part, wrow, wcol, grow, gcol, w_value):
    lcoord = coord_unit(grow)
    mcoord = coord_unit(gcol)
    angle = w_value * (lcoord[:, None] ** 2 + mcoord[None, :] ** 2)
    scale = wrow[:, None] * wcol[None, :]
    first = real_part.astype(jnp.float32) * scale
    second = imag_part.astype(jnp.float32) * scale
    cosine = jnp.cos(angle)
    sine = jnp.sin(angle)
    return ((first * cosine - second * sine).astype(jnp.bfloat16), (first * sine + second * cosine).astype(jnp.bfloat16))

def matmul(left, right):
    return jnp.dot(left.astype(jnp.float32), right.astype(jnp.float32), precision=lax.Precision.HIGHEST)

def reference(image, window_rows, window_cols, w_terms, facet_row_offset, facet_col_offset, band_offset, sub_row_offset, sub_column):
    local = jnp.arange(F, dtype=jnp.int32)
    freq_base = jnp.arange(SG, dtype=jnp.int32)

    def row_step(total, row_index):
        wrow = lax.dynamic_slice(window_rows, ((row_index * F).astype(jnp.int32),), (F,))
        grow = facet_row_offset[row_index] + local

        def col_step(acc, col_index):
            pixels = lax.dynamic_slice(image, (jnp.int32(0), (row_index * F).astype(jnp.int32), (col_index * F).astype(jnp.int32)), (2, F, F))
            wcol = lax.dynamic_slice(window_cols, ((col_index * F).astype(jnp.int32),), (F,))
            gcol = facet_col_offset[col_index] + local
            pieces = []
            for column in range(COLS):
                prep_re, prep_im = prepare(pixels[0], pixels[1], wrow, wcol, grow, gcol, w_terms[column])
                table_re, table_im = dft_table(gcol[:, None], band_offset[column] + freq_base[None, :])
                out_re = matmul(prep_re, table_re) - matmul(prep_im, table_im)
                out_im = matmul(prep_re, table_im) + matmul(prep_im, table_re)
                pieces.append(jnp.stack([out_re, out_im], axis=1))
            return (acc + jnp.stack(pieces, axis=1), None)
        summed, _ = lax.scan(col_step, jnp.zeros((F, COLS, 2, SG), jnp.float32), jnp.arange(N_FCOL, dtype=jnp.int32))
        banded = (summed / math.sqrt(NY)).astype(jnp.bfloat16)
        results = []
        for sub_index in range(SUB):
            table_re, table_im = dft_table(grow[:, None], sub_row_offset[sub_index] + freq_base[None, :])
            chosen = banded[:, sub_column[sub_index]]
            band_re = chosen[:, 0]
            band_im = chosen[:, 1]
            out_re = matmul(table_re.T, band_re) - matmul(table_im.T, band_im)
            out_im = matmul(table_re.T, band_im) + matmul(table_im.T, band_re)
            results.append(jnp.stack([out_re, out_im], axis=0))
        return (total + jnp.stack(results, axis=0) / math.sqrt(NX), None)
    subgrids, _ = lax.scan(row_step, jnp.zeros((SUB, 2, SG, SG), jnp.float32), jnp.arange(N_FROW, dtype=jnp.int32))
    return subgrids
```

```python
import functools
import math

import jax
import jax.numpy as jnp
from jax import lax
from jax.experimental import pallas as pl
from jax.experimental.pallas import tpu as pltpu
from jax.sharding import Mesh
from jax.sharding import PartitionSpec as P

IMAGE = 65536
F = 512
f32 = jnp.float32
bf16 = jnp.bfloat16
FROW = ("zh", "y")
FCOL = ("zl", "x", "c")
Z = ("zh", "zl")
PIO2 = (1.5703125, 4.837512969970703125e-4, 7.549789948768648e-8)
NT = (((1,), (1,)), ((), ()))
NN = (((1,), (0,)), ((), ()))


def sincos_of(r, q):
    z = r * r
    s = r + r * z * (-1.6666654611e-1 + z * (8.3321608736e-3 - 1.9515295891e-4 * z))
    c = 1.0 - 0.5 * z + z * z * (4.166664568298827e-2 + z * (-1.388731625493765e-3 + 2.443315711809948e-5 * z))
    odd = (q & 1) == 1
    cosine = jnp.where(odd, s, c)
    sine = jnp.where(odd, c, s)
    cosine = jnp.where(((q + 1) & 2) == 2, -cosine, cosine)
    sine = jnp.where((q & 2) == 2, -sine, sine)
    return cosine, sine


def turn(p):
    q = (p + 8192) >> 14
    r = (p - (q << 14)).astype(f32) * (2.0 * math.pi / IMAGE)
    c, s = sincos_of(r, q)
    return c, -s


def phase_index(first, second):
    high = ((first * (second >> 8)) & 255) << 8
    return (high + first * (second & 255)) & (IMAGE - 1)


def chirp(w, g):
    unit = (g & (IMAGE - 1)).astype(f32) * (1.0 / IMAGE) - 0.5
    angle = w * (unit * unit)
    n = jnp.floor(angle * (2.0 / math.pi) + 0.5)
    r = ((angle - n * PIO2[0]) - n * PIO2[1]) - n * PIO2[2]
    return sincos_of(r, n.astype(jnp.int32))


def times(a, b):
    return a[0] * b[0] - a[1] * b[1], a[0] * b[1] + a[1] * b[0]


def ids():
    return {name: lax.axis_index(name) for name in ("zh", "y", "zl", "x", "c")}


def outer(a, b):
    n = a[0].shape[1]
    big = [v[:, None, :] for v in a]
    small = [v[None, :, :] for v in b]
    return [v.reshape(-1, n) for v in times(big, small)]


def column_factors(at, w, band, offset, window):
    g = offset + lax.broadcasted_iota(jnp.int32, (1, F), 1)
    i = lax.broadcasted_iota(jnp.int32, (16, F), 0)
    zl = (at["zl"] + (i >> 3)) & 1
    x = (at["x"] + (i >> 1)) & 3
    c = (at["c"] + i) & 1
    coarse = turn(phase_index(g, band + ((zl * 4 + x) * 2 + c) * 32))
    wave = chirp(w, g)
    coarse = times(coarse, (wave[0] * window, wave[1] * window))
    fine = turn((g * lax.broadcasted_iota(jnp.int32, (32, F), 0)) & (IMAGE - 1))
    return coarse, fine


def column_table(factors, t):
    coarse, fine = factors
    re, im = outer([v[2 * t : 2 * t + 2] for v in coarse], fine)
    first = jnp.concatenate([re, im], axis=0).astype(bf16)
    second = jnp.concatenate([-im, re], axis=0).astype(bf16)
    return first, second


def scalars(at, w_terms, band_offset, sub_column):
    column = sub_column[at["c"]]
    return w_terms[column], band_offset[column]


def own_kernel(w_terms, fro, fco, bo, sro, sc, image, wrow, wcol, rt, g_out, w1, w2):
    at = ids()
    w, band = scalars(at, w_terms, bo, sc)
    me = (at["zl"] * 4 + at["x"]) * 2 + at["c"]
    factors = column_factors(at, w, band, fco[me], wcol[...])
    for t in range(8):
        rows = pl.ds(t * 128, 128)
        w1[rows, :], w2[rows, :] = column_table(factors, t)
    for n in range(4):
        rows = pl.ds(n * 256, 256)
        g_out[:, rows] = lax.dot_general(image[0], w1[rows, :], NT, preferred_element_type=f32) + lax.dot_general(
            image[1], w2[rows, :], NT, preferred_element_type=f32
        )
    g = fro[at["zh"] * 4 + at["y"]] + lax.broadcasted_iota(jnp.int32, (1, F), 1)
    i = lax.broadcasted_iota(jnp.int32, (16, F), 0)
    wave = chirp(w, g)
    window = wrow[...] * (1.0 / 8192.0)
    wave = (wave[0] * window, wave[1] * window)
    first = sro[at["c"]]
    fine = turn((g * lax.broadcasted_iota(jnp.int32, (32, F), 0)) & (IMAGE - 1))

    def coarse_rows(base):
        block = ((base + i) & 3) * 4 + ((at["y"] + (i >> 2)) & 3)
        return times(turn(phase_index(g, first + block * 32)), wave)

    plain = coarse_rows(at["zh"])
    moved = coarse_rows(at["zh"] + at["zl"])
    for part in range(4):
        re, im = outer(moved if part == 3 else plain, [v[part * 8 : part * 8 + 8] for v in fine])
        rt[pl.ds(part * 128, 128), pl.ds(0, F)] = re.astype(bf16)
        rt[pl.ds(part * 128, 128), pl.ds(F, F)] = im.astype(bf16)


def other_kernel(w_terms, fco, bo, sc, wcol, w1, w2):
    at = ids()
    w, band = scalars(at, w_terms, bo, sc)
    me = (at["zl"] * 4 + at["x"]) * 2 + (1 - at["c"])
    factors = column_factors(at, w, band, fco[me], wcol[...])
    for t in range(8):
        rows = pl.ds(t * 128, 128)
        w1[rows, :], w2[rows, :] = column_table(factors, t)


def sum_kernel(rt, g_own, w1, w2, image, *rest):
    xo, yo, z1, z2 = rest[0:4], rest[4:8], rest[8:10], rest[10:12]
    gg, im = rest[12:]
    im[0] = image[0].astype(bf16)
    im[1] = image[1].astype(bf16)
    sign = jnp.where(lax.broadcasted_iota(jnp.int32, (1, 128), 1) < 64, -1.0, 1.0)
    for n in range(4):
        rows = pl.ds(n * 256, 256)
        g = g_own[:, rows] + lax.dot_general(im[0], w1[rows, :], NT, preferred_element_type=f32)
        g = g + lax.dot_general(im[1], w2[rows, :], NT, preferred_element_type=f32)
        gg[pl.ds(0, F), rows] = g.astype(bf16)
        for h in range(2):
            half = pltpu.roll(g[:, h * 128 : h * 128 + 128], 64, 1) * sign
            gg[pl.ds(F, F), pl.ds(n * 256 + h * 128, 128)] = half.astype(bf16)
    for n in range(4):
        s = lax.dot_general(rt[...], gg[:, pl.ds(n * 256, 256)], NN, preferred_element_type=f32)
        for h in range(2):
            t = 2 * n + h
            zl, x = t // 4, t % 4
            piece = s[:, h * 128 : h * 128 + 128]
            xo[x][:, pl.ds(zl * 128, 128)] = piece[0:128]
            for y in range(4):
                yo[y][:, pl.ds(t * 128, 128)] = piece[128 + y * 32 : 160 + y * 32]
            z1[zl][:, pl.ds(x * 128, 128)] = piece[256:384]
            z2[zl][:, pl.ds(x * 128, 128)] = piece[384:512]


def shift(value, axis, step):
    n = lax.axis_size(axis)
    return lax.ppermute(value, axis, [(i, (i + step) % n) for i in range(n)])


def sent_round(pieces, axis):
    total = pieces[0]
    for step, piece in enumerate(pieces[1:], 1):
        total = total + shift(piece, axis, step)
    return total


def rows_of(value, count):
    size = value.shape[0] // count
    return [value[i * size : (i + 1) * size] for i in range(count)]


def cols_of(value, count):
    size = value.shape[1] // count
    return [value[:, i * size : (i + 1) * size] for i in range(count)]


def local(image, wrow, wcol, w_terms, fro, fco, bo, sro, sc):
    smem = pl.BlockSpec(memory_space=pltpu.SMEM)
    vmem = pl.BlockSpec(memory_space=pltpu.VMEM)
    params = pltpu.CompilerParams(vmem_limit_bytes=24 * 2**20)
    swap = [(0, 1), (1, 0)]
    window = wcol.reshape(1, F)
    other_window = lax.ppermute(window, "c", swap)
    other_image = lax.ppermute(image.astype(f32), "c", swap)
    table = jax.ShapeDtypeStruct((2 * F, F), bf16)
    rt, g_own = pl.pallas_call(
        own_kernel,
        out_shape=(jax.ShapeDtypeStruct((F, 2 * F), bf16), jax.ShapeDtypeStruct((F, 2 * F), f32)),
        in_specs=[smem] * 6 + [vmem] * 3,
        out_specs=(vmem, vmem),
        scratch_shapes=[pltpu.VMEM((2 * F, F), bf16)] * 2,
        compiler_params=params,
        cost_estimate=pl.CostEstimate(flops=2**30, bytes_accessed=4 * 2**20, transcendentals=0),
        name="own_facet",
    )(w_terms, fro, fco, bo, sro, sc, image, wrow.reshape(1, F), window)
    w1, w2 = pl.pallas_call(
        other_kernel,
        out_shape=(table, table),
        in_specs=[smem] * 4 + [vmem],
        out_specs=(vmem, vmem),
        compiler_params=params,
        cost_estimate=pl.CostEstimate(flops=2**22, bytes_accessed=2 * 2**20, transcendentals=0),
        name="other_table",
    )(w_terms, fco, bo, sc, other_window)
    shapes = [(128, 256)] * 4 + [(32, 1024)] * 4 + [(128, 512)] * 4
    pieces = pl.pallas_call(
        sum_kernel,
        out_shape=[jax.ShapeDtypeStruct(s, f32) for s in shapes],
        in_specs=[vmem] * 5,
        out_specs=[vmem] * 12,
        scratch_shapes=[pltpu.VMEM((2 * F, 2 * F), bf16), pltpu.VMEM((2, F, F), bf16)],
        compiler_params=params,
        cost_estimate=pl.CostEstimate(flops=2**31, bytes_accessed=9 * 2**20, transcendentals=0),
        name="two_stages",
    )(rt, g_own, w1, w2, other_image)
    xs, ys, z1, z2 = pieces[0:4], pieces[4:8], pieces[8:10], pieces[10:12]
    nearby = [(z, (z + 1 if z % 2 else z - 1) % 8) for z in range(8)]
    part_z1 = sent_round(z1, "zl")
    part_z2 = z2[0] + lax.ppermute(z2[1], Z, nearby)
    part_x = sent_round(xs, "x")
    part_y = sent_round(ys, "y")
    part_z1 = sent_round(cols_of(part_z1, 4), "x")
    part_z2 = sent_round(rows_of(part_z2, 4), "y")
    part_x = sent_round(cols_of(part_x, 2), "zl")
    part_y = sent_round(cols_of(part_y, 2), "zl")
    part_x = sent_round(rows_of(part_x, 4), "y")
    part_z1 = sent_round(rows_of(part_z1, 4), "y")
    part_y = sent_round(cols_of(part_y, 4), "x")
    part_z2 = sent_round(cols_of(part_z2, 4), "x")
    part_z2 = jnp.where(lax.axis_index("zl") == 1, jnp.roll(part_z2, 8, axis=0), part_z2)
    whole = jnp.stack([v.reshape(4, 8, 2, 2, 32) for v in (part_x, part_y, part_z1, part_z2)], axis=1)
    whole = whole.reshape(4, 32, 2, 2, 32)
    core = "c"

    def routed(value, step, cross):
        if not (step or cross):
            return value
        perm = [(z * 2 + c, (z + step) % 4 * 2 + (c ^ cross)) for z in range(4) for c in range(2)]
        return lax.ppermute(value, ("zh", core), perm)

    sums = [sum(routed(whole[r, :, :, cross], r, cross) for r in range(4)) for cross in (0, 1)]
    mine, theirs = [v.transpose(1, 0, 2) for v in sums]
    first = lax.axis_index(core) == 0
    return jnp.stack([jnp.where(first, mine, theirs), jnp.where(first, theirs, mine)])


def solution(mesh):
    torus = Mesh(mesh.devices.reshape(4, 4, 2, 4, 2), ("zh", "y", "zl", "x", "c"))
    placed = (P(None, FROW, FCOL), P(FROW), P(FCOL), P(), P(), P(), P(), P(), P())
    return jax.shard_map(local, mesh=torus, in_specs=placed, out_specs=P(None, None, FROW, FCOL), check_vma=False)
```

```python
import itertools
import math

import jax
import jax.numpy as jnp
from jax import lax
from jax.experimental import pallas as pl
from jax.experimental.pallas import tpu as pltpu
from jax.sharding import Mesh
from jax.sharding import PartitionSpec as P

IMAGE = 65536
F = 512
f32 = jnp.float32
bf16 = jnp.bfloat16
FROW = ("zh", "y")
FCOL = ("zl", "x", "c")
Z = ("zh", "zl")
PIO2 = (1.5703125, 4.837512969970703125e-4, 7.549789948768648e-8)
NT = (((1,), (1,)), ((), ()))
NN = (((1,), (0,)), ((), ()))


def sincos_of(r, q):
    z = r * r
    s = r + r * z * (-1.6666654611e-1 + z * (8.3321608736e-3 - 1.9515295891e-4 * z))
    c = 1.0 - 0.5 * z + z * z * (4.166664568298827e-2 + z * (-1.388731625493765e-3 + 2.443315711809948e-5 * z))
    odd = (q & 1) == 1
    cosine = jnp.where(odd, s, c)
    sine = jnp.where(odd, c, s)
    cosine = jnp.where(((q + 1) & 2) == 2, -cosine, cosine)
    sine = jnp.where((q & 2) == 2, -sine, sine)
    return cosine, sine


def turn(p):
    q = (p + 8192) >> 14
    r = (p - (q << 14)).astype(f32) * (2.0 * math.pi / IMAGE)
    c, s = sincos_of(r, q)
    return c, -s


def phase_index(first, second):
    high = ((first * (second >> 8)) & 255) << 8
    return (high + first * (second & 255)) & (IMAGE - 1)


def chirp(w, g):
    unit = (g & (IMAGE - 1)).astype(f32) * (1.0 / IMAGE) - 0.5
    angle = w * (unit * unit)
    n = jnp.floor(angle * (2.0 / math.pi) + 0.5)
    r = ((angle - n * PIO2[0]) - n * PIO2[1]) - n * PIO2[2]
    return sincos_of(r, n.astype(jnp.int32))


def times(a, b):
    return a[0] * b[0] - a[1] * b[1], a[0] * b[1] + a[1] * b[0]


def ids():
    return {name: lax.axis_index(name) for name in ("zh", "y", "zl", "x", "c")}


def outer(a, b):
    n = a[0].shape[1]
    big = [v[:, None, :] for v in a]
    small = [v[None, :, :] for v in b]
    return [v.reshape(-1, n) for v in times(big, small)]


def gray(i):
    return i ^ (i >> 1)


def near(own, high, low, core):
    low_first = high | (low << 1)
    high_first = low | (high << 1)
    return gray(gray(own) ^ jnp.where(core == 0, low_first, high_first))


def per_sub(sub, values):
    return jnp.where(sub == 0, values[0], values[1])


def column_factors(at, w_terms, bo, sc, offset, window):
    g = offset + lax.broadcasted_iota(jnp.int32, (1, F), 1)
    i = lax.broadcasted_iota(jnp.int32, (16, F), 0)
    x = near(at["x"], i >> 3, (i >> 2) & 1, at["c"])
    sub = (i >> 1) & 1
    zl = at["zl"] ^ (i & 1)
    band = per_sub(sub, [bo[sc[k]] for k in range(2)])
    coarse = turn(phase_index(g, band + ((zl * 4 + x) * 2 + at["c"]) * 32))
    waves = [chirp(w_terms[sc[k]], g) for k in range(2)]
    wave = [per_sub(sub, [v[part] * window for v in waves]) for part in range(2)]
    coarse = times(coarse, wave)
    fine = turn((g * lax.broadcasted_iota(jnp.int32, (32, F), 0)) & (IMAGE - 1))
    return coarse, fine


def column_table(factors, t):
    coarse, fine = factors
    first, second = [], []
    for zl in range(2):
        row = 2 * t + zl
        re, im = outer([v[row : row + 1] for v in coarse], fine)
        first += [re, im]
        second += [-im, re]
    return [jnp.concatenate(v, axis=0).astype(bf16) for v in (first, second)]


def own_kernel(w_terms, fro, fco, bo, sro, sc, image, wrow, wcol, rt, g_out, w1, w2):
    at = ids()
    me = (at["zl"] * 4 + at["x"]) * 2 + at["c"]
    factors = column_factors(at, w_terms, bo, sc, fco[me], wcol[...])
    for t in range(8):
        rows = pl.ds(t * 128, 128)
        w1[rows, :], w2[rows, :] = column_table(factors, t)
    for n in range(4):
        rows = pl.ds(n * 256, 256)
        g_out[:, rows] = lax.dot_general(image[0], w1[rows, :], NT, preferred_element_type=f32) + lax.dot_general(
            image[1], w2[rows, :], NT, preferred_element_type=f32
        )
    g = fro[at["zh"] * 4 + at["y"]] + lax.broadcasted_iota(jnp.int32, (1, F), 1)
    i = lax.broadcasted_iota(jnp.int32, (16, F), 0)
    window = wrow[...] * (1.0 / 8192.0)
    fine = turn((g * lax.broadcasted_iota(jnp.int32, (32, F), 0)) & (IMAGE - 1))
    y = near(at["y"], i >> 3, (i >> 2) & 1, at["c"])
    zh = near(at["zh"], (i >> 1) & 1, i & 1, at["c"])
    for k in range(2):
        wave = [v * window for v in chirp(w_terms[sc[k]], g)]
        coarse = times(turn(phase_index(g, sro[k] + (zh * 4 + y) * 32)), wave)
        for part in range(2):
            re, im = outer(coarse, [v[part * 16 : part * 16 + 16] for v in fine])
            rt[k, pl.ds(part * 256, 256), pl.ds(0, F)] = re.astype(bf16)
            rt[k, pl.ds(part * 256, 256), pl.ds(F, F)] = im.astype(bf16)


def other_kernel(w_terms, fco, bo, sc, wcol, w1, w2):
    at = ids()
    me = (at["zl"] * 4 + at["x"]) * 2 + (1 - at["c"])
    factors = column_factors(at, w_terms, bo, sc, fco[me], wcol[...])
    for t in range(8):
        rows = pl.ds(t * 128, 128)
        w1[rows, :], w2[rows, :] = column_table(factors, t)


def sum_kernel(rt, g_own, w1, w2, image, a_keep, a_send, b_keep, b_send, gg, im):
    im[0] = image[0].astype(bf16)
    im[1] = image[1].astype(bf16)
    imag = (lax.broadcasted_iota(jnp.int32, (F, 128), 1) & 32) == 32
    for n in range(4):
        rows = pl.ds(n * 256, 256)
        g = g_own[:, rows] + lax.dot_general(im[0], w1[rows, :], NT, preferred_element_type=f32)
        g = g + lax.dot_general(im[1], w2[rows, :], NT, preferred_element_type=f32)
        for k in range(2):
            tile = g[:, k * 128 : k * 128 + 128]
            turned = jnp.where(imag, pltpu.roll(tile, 32, 1), -pltpu.roll(tile, 96, 1))
            cols = pl.ds(n * 128, 128)
            gg[k, pl.ds(0, F), cols] = tile.astype(bf16)
            gg[k, pl.ds(F, F), cols] = turned.astype(bf16)
    for k in range(2):
        for half in range(2):
            s = lax.dot_general(rt[k], gg[k, :, pl.ds(half * 256, 256)], NN, preferred_element_type=f32)
            a_out = a_send if half else a_keep
            for low in range(2):
                tile = s[:, low * 128 : low * 128 + 128]
                a_out[:, pl.ds(low * 256 + k * 128, 128)] = tile[0:256]
                cols = pl.ds(half * 512 + low * 256 + k * 128, 128)
                b_keep[:, cols] = tile[256:384]
                b_send[:, cols] = tile[384:512]


def partner(place, bit):
    zh, y, zl, x, c = place
    if bit[0] == "z":
        if bit == "zl":
            return zh, y, zl ^ 1, x, c
        return gray(gray(zh) ^ "ab".index(bit[1]) + 1), y, zl, x, c
    flip = "ab".index(bit[1]) + 1
    if bit[0] == "x":
        return zh, y, zl, gray(gray(x) ^ flip), c
    return zh, gray(gray(y) ^ flip), zl, x, c


def swapped(value, axis, order):
    sizes = (4, 4, 2, 4, 2)
    places = list(itertools.product(*map(range, sizes)))
    number = {place: i for i, place in enumerate(places)}
    perm = [(i, number[partner(p, axis + order[p[-1]])]) for i, p in enumerate(places)]
    return lax.ppermute(value, ("zh", "y", "zl", "x", "c"), perm)


def local(image, wrow, wcol, w_terms, fro, fco, bo, sro, sc):
    smem = pl.BlockSpec(memory_space=pltpu.SMEM)
    vmem = pl.BlockSpec(memory_space=pltpu.VMEM)
    params = pltpu.CompilerParams(vmem_limit_bytes=24 * 2**20)
    swap = [(0, 1), (1, 0)]
    window = wcol.reshape(1, F)
    other_window = lax.ppermute(window, "c", swap)
    other_image = lax.ppermute(image.astype(f32), "c", swap)
    table = jax.ShapeDtypeStruct((2 * F, F), bf16)
    rt, g_own = pl.pallas_call(
        own_kernel,
        out_shape=(jax.ShapeDtypeStruct((2, F, 2 * F), bf16), jax.ShapeDtypeStruct((F, 2 * F), f32)),
        in_specs=[smem] * 6 + [vmem] * 3,
        out_specs=(vmem, vmem),
        scratch_shapes=[pltpu.VMEM((2 * F, F), bf16)] * 2,
        compiler_params=params,
        cost_estimate=pl.CostEstimate(flops=2**30, bytes_accessed=4 * 2**20, transcendentals=0),
        name="own_facet",
    )(w_terms, fro, fco, bo, sro, sc, image, wrow.reshape(1, F), window)
    w1, w2 = pl.pallas_call(
        other_kernel,
        out_shape=(table, table),
        in_specs=[smem] * 4 + [vmem],
        out_specs=(vmem, vmem),
        compiler_params=params,
        cost_estimate=pl.CostEstimate(flops=2**22, bytes_accessed=2 * 2**20, transcendentals=0),
        name="other_table",
    )(w_terms, fco, bo, sc, other_window)
    shapes = [(256, 512)] * 2 + [(128, 1024)] * 2
    a_keep, a_send, b_keep, b_send = pl.pallas_call(
        sum_kernel,
        out_shape=[jax.ShapeDtypeStruct(s, f32) for s in shapes],
        in_specs=[vmem] * 5,
        out_specs=[vmem] * 4,
        scratch_shapes=[pltpu.VMEM((2, 2 * F, F), bf16), pltpu.VMEM((2, F, F), bf16)],
        compiler_params=params,
        cost_estimate=pl.CostEstimate(flops=2**31, bytes_accessed=9 * 2**20, transcendentals=0),
        name="two_stages",
    )(rt, g_own, w1, w2, other_image)
    a = a_keep + swapped(a_send, "x", "ab")
    b = b_keep + swapped(b_send, "y", "ab")
    a = a[:128] + swapped(a[128:], "y", "ab")
    b = b[:, :512] + swapped(b[:, 512:], "x", "ab")
    whole = jnp.stack([a.reshape(2, 64, 512), b.reshape(2, 64, 512)], axis=1).reshape(256, 512)
    whole = whole[:, :256] + swapped(whole[:, 256:], "x", "ba")
    whole = whole[:128] + swapped(whole[128:], "y", "ba")
    whole = whole.reshape(2, 2, 2, 16, 256)
    whole = whole[:, 0] + swapped(whole[:, 1], "z", "ab")
    whole = whole[:, 0] + swapped(whole[:, 1], "z", "ba")
    whole = whole.reshape(32, 2, 2, 64)
    whole = whole[:, :, 0] + swapped(whole[:, :, 1], "z", "ll")
    return whole.reshape(32, 2, 2, 32).transpose(1, 2, 0, 3)


def solution(mesh):
    torus = Mesh(mesh.devices.reshape(4, 4, 2, 4, 2), ("zh", "y", "zl", "x", "c"))
    placed = (P(None, FROW, FCOL), P(FROW), P(FCOL), P(), P(), P(), P(), P(), P())
    return jax.shard_map(local, mesh=torus, in_specs=placed, out_specs=P(None, None, FROW, FCOL), check_vma=False)
```

```python
import itertools
import math

import jax
import jax.numpy as jnp
from jax import lax
from jax.experimental import pallas as pl
from jax.experimental.pallas import tpu as pltpu
from jax.sharding import Mesh
from jax.sharding import PartitionSpec as P

IMAGE = 65536
F = 512
f32 = jnp.float32
bf16 = jnp.bfloat16
FROW = ("zh", "y")
FCOL = ("zl", "x", "c")
Z = ("zh", "zl")
PIO2 = (1.5703125, 4.837512969970703125e-4, 7.549789948768648e-8)
NT = (((1,), (1,)), ((), ()))
NN = (((1,), (0,)), ((), ()))


def sincos_of(r, q):
    z = r * r
    s = r + r * z * (-1.6666654611e-1 + z * (8.3321608736e-3 - 1.9515295891e-4 * z))
    c = 1.0 - 0.5 * z + z * z * (4.166664568298827e-2 + z * (-1.388731625493765e-3 + 2.443315711809948e-5 * z))
    odd = (q & 1) == 1
    cosine = jnp.where(odd, s, c)
    sine = jnp.where(odd, c, s)
    cosine = jnp.where(((q + 1) & 2) == 2, -cosine, cosine)
    sine = jnp.where((q & 2) == 2, -sine, sine)
    return cosine, sine


def turn(p):
    q = (p + 8192) >> 14
    r = (p - (q << 14)).astype(f32) * (2.0 * math.pi / IMAGE)
    c, s = sincos_of(r, q)
    return c, -s


def phase_index(first, second):
    high = ((first * (second >> 8)) & 255) << 8
    return (high + first * (second & 255)) & (IMAGE - 1)


def chirp(w, g):
    unit = (g & (IMAGE - 1)).astype(f32) * (1.0 / IMAGE) - 0.5
    angle = w * (unit * unit)
    n = jnp.floor(angle * (2.0 / math.pi) + 0.5)
    r = ((angle - n * PIO2[0]) - n * PIO2[1]) - n * PIO2[2]
    return sincos_of(r, n.astype(jnp.int32))


def times(a, b):
    return a[0] * b[0] - a[1] * b[1], a[0] * b[1] + a[1] * b[0]


def ids():
    return {name: lax.axis_index(name) for name in ("zh", "y", "zl", "x", "c")}


def outer(a, b):
    n = a[0].shape[1]
    big = [v[:, None, :] for v in a]
    small = [v[None, :, :] for v in b]
    return [v.reshape(-1, n) for v in times(big, small)]


def gray(i):
    return i ^ (i >> 1)


def near(own, high, low, core):
    low_first = high | (low << 1)
    high_first = low | (high << 1)
    return gray(gray(own) ^ jnp.where(core == 0, low_first, high_first))


def per_sub(sub, values):
    return jnp.where(sub == 0, values[0], values[1])


def column_factors(at, w_terms, bo, sc, offset, window):
    g = offset + lax.broadcasted_iota(jnp.int32, (1, F), 1)
    i = lax.broadcasted_iota(jnp.int32, (16, F), 0)
    x = near(at["x"], i >> 3, (i >> 2) & 1, at["c"])
    sub = (i >> 1) & 1
    zl = i & 1
    band = per_sub(sub, [bo[sc[k]] for k in range(2)])
    coarse = turn(phase_index(g, band + ((zl * 4 + x) * 2 + at["c"]) * 32))
    waves = [chirp(w_terms[sc[k]], g) for k in range(2)]
    wave = [per_sub(sub, [v[part] * window for v in waves]) for part in range(2)]
    coarse = times(coarse, wave)
    fine = turn((g * lax.broadcasted_iota(jnp.int32, (32, F), 0)) & (IMAGE - 1))
    return coarse, fine


def column_table(factors, t):
    coarse, fine = factors
    first, second = [], []
    for zl in range(2):
        row = 2 * t + zl
        re, im = outer([v[row : row + 1] for v in coarse], fine)
        first += [re, im]
        second += [-im, re]
    return [jnp.concatenate(v, axis=0).astype(bf16) for v in (first, second)]


def own_kernel(w_terms, fro, fco, bo, sro, sc, image, wrow, wcol, rt, g_out, w1, w2):
    at = ids()
    me = (at["zl"] * 4 + at["x"]) * 2 + at["c"]
    factors = column_factors(at, w_terms, bo, sc, fco[me], wcol[...])
    for t in range(8):
        rows = pl.ds(t * 128, 128)
        w1[rows, :], w2[rows, :] = column_table(factors, t)
    for n in range(4):
        rows = pl.ds(n * 256, 256)
        g_out[:, rows] = lax.dot_general(image[0], w1[rows, :], NT, preferred_element_type=f32) + lax.dot_general(
            image[1], w2[rows, :], NT, preferred_element_type=f32
        )
    g = fro[at["zh"] * 4 + at["y"]] + lax.broadcasted_iota(jnp.int32, (1, F), 1)
    i = lax.broadcasted_iota(jnp.int32, (16, F), 0)
    window = wrow[...] * (1.0 / 8192.0)
    fine = turn((g * lax.broadcasted_iota(jnp.int32, (32, F), 0)) & (IMAGE - 1))
    y = near(at["y"], i >> 3, (i >> 2) & 1, at["c"])
    zh = i & 3
    for k in range(2):
        wave = [v * window for v in chirp(w_terms[sc[k]], g)]
        coarse = times(turn(phase_index(g, sro[k] + (zh * 4 + y) * 32)), wave)
        re, im = outer(coarse, fine)
        rt[k, :, pl.ds(0, F)] = re.astype(bf16)
        rt[k, :, pl.ds(F, F)] = im.astype(bf16)


def other_kernel(w_terms, fco, bo, sc, wcol, w1, w2):
    at = ids()
    me = (at["zl"] * 4 + at["x"]) * 2 + (1 - at["c"])
    factors = column_factors(at, w_terms, bo, sc, fco[me], wcol[...])
    for t in range(8):
        rows = pl.ds(t * 128, 128)
        w1[rows, :], w2[rows, :] = column_table(factors, t)


def sum_kernel(rt, g_own, w1, w2, image, keep, to_x, to_y, to_xy, gg, im):
    im[0] = image[0].astype(bf16)
    im[1] = image[1].astype(bf16)
    imag = (lax.broadcasted_iota(jnp.int32, (F, 128), 1) & 32) == 32
    for n in range(4):
        rows = pl.ds(n * 256, 256)
        g = g_own[:, rows] + lax.dot_general(im[0], w1[rows, :], NT, preferred_element_type=f32)
        g = g + lax.dot_general(im[1], w2[rows, :], NT, preferred_element_type=f32)
        for k in range(2):
            tile = g[:, k * 128 : k * 128 + 128]
            turned = jnp.where(imag, pltpu.roll(tile, 32, 1), -pltpu.roll(tile, 96, 1))
            cols = pl.ds(n * 128, 128)
            gg[k, pl.ds(0, F), cols] = tile.astype(bf16)
            gg[k, pl.ds(F, F), cols] = turned.astype(bf16)
    for k in range(2):
        for half in range(2):
            s = lax.dot_general(rt[k], gg[k, :, pl.ds(half * 256, 256)], NN, preferred_element_type=f32)
            for low in range(2):
                tile = s[:, low * 128 : low * 128 + 128]
                cols = pl.ds(low * 256 + k * 128, 128)
                (to_x if half else keep)[:, cols] = tile[:256]
                (to_xy if half else to_y)[:, cols] = tile[256:]


def swapped(value, axes, second):
    places = list(itertools.product(*map(range, (4, 4, 2, 4, 2))))
    number = {place: i for i, place in enumerate(places)}
    perm = []
    for i, (zh, y, zl, x, c) in enumerate(places):
        flip = 1 + (c ^ second)
        if "x" in axes:
            x = gray(gray(x) ^ flip)
        if "y" in axes:
            y = gray(gray(y) ^ flip)
        perm.append((i, number[zh, y, zl, x, c]))
    return lax.ppermute(value, ("zh", "y", "zl", "x", "c"), perm)


def arrived(pieces, second):
    return [pieces[0]] + [swapped(v, axes, second) for v, axes in zip(pieces[1:], ("x", "y", "xy"))]


def cut_kernel(own, by_x, by_y, by_xy, keep, to_x, to_y, to_xy):
    for y in range(2):
        for x in range(2):
            rows, cols = pl.ds(y * 128, 128), pl.ds(x * 256, 256)
            total = (own[rows, cols] + by_x[rows, cols]) + (by_y[rows, cols] + by_xy[rows, cols])
            ((keep, to_x), (to_y, to_xy))[y][x][...] = total


def pack_kernel(own, by_x, by_y, by_xy, out):
    low = lax.broadcasted_iota(jnp.int32, (128, 128), 1) < 64
    total = (own[...] + by_x[...]) + (by_y[...] + by_xy[...])
    one, two = total[:, :128], total[:, 128:]
    left = jnp.where(low, one, pltpu.roll(two, 64, 1))
    right = jnp.where(low, pltpu.roll(one, 64, 1), two)
    for zh in range(4):
        rows = slice(zh * 32, zh * 32 + 32)
        out[2 * zh] = left[rows]
        out[2 * zh + 1] = right[rows]


def last_kernel(pieces, out):
    total = jnp.sum(pieces[...], axis=0)
    for k in range(2):
        for c in range(2):
            out[k, c] = total[:, (2 * k + c) * 32 : (2 * k + c) * 32 + 32]


def spread(pieces):
    vmem = pl.BlockSpec(memory_space=pltpu.VMEM)
    params = pltpu.CompilerParams(vmem_limit_bytes=8 * 2**20)
    pieces = pl.pallas_call(
        cut_kernel,
        out_shape=[jax.ShapeDtypeStruct((128, 256), f32)] * 4,
        in_specs=[vmem] * 4,
        out_specs=[vmem] * 4,
        compiler_params=params,
        name="cut",
    )(*arrived(pieces, 0))
    packed = pl.pallas_call(
        pack_kernel,
        out_shape=jax.ShapeDtypeStruct((8, 32, 128), f32),
        in_specs=[vmem] * 4,
        out_specs=vmem,
        compiler_params=params,
        name="pack",
    )(*arrived(pieces, 1))
    blocks = lax.all_to_all(packed, ("zh", "zl"), 0, 0, tiled=True)
    return pl.pallas_call(
        last_kernel,
        out_shape=jax.ShapeDtypeStruct((2, 2, 32, 32), f32),
        in_specs=[vmem],
        out_specs=vmem,
        compiler_params=params,
        name="last_sum",
    )(blocks)


def local(image, wrow, wcol, w_terms, fro, fco, bo, sro, sc):
    smem = pl.BlockSpec(memory_space=pltpu.SMEM)
    vmem = pl.BlockSpec(memory_space=pltpu.VMEM)
    params = pltpu.CompilerParams(vmem_limit_bytes=24 * 2**20)
    swap = [(0, 1), (1, 0)]
    window = wcol.reshape(1, F)
    other_window = lax.ppermute(window, "c", swap)
    other_image = lax.ppermute(image.astype(f32), "c", swap)
    table = jax.ShapeDtypeStruct((2 * F, F), bf16)
    rt, g_own = pl.pallas_call(
        own_kernel,
        out_shape=(jax.ShapeDtypeStruct((2, F, 2 * F), bf16), jax.ShapeDtypeStruct((F, 2 * F), f32)),
        in_specs=[smem] * 6 + [vmem] * 3,
        out_specs=(vmem, vmem),
        scratch_shapes=[pltpu.VMEM((2 * F, F), bf16)] * 2,
        compiler_params=params,
        cost_estimate=pl.CostEstimate(flops=2**30, bytes_accessed=4 * 2**20, transcendentals=0),
        name="own_facet",
    )(w_terms, fro, fco, bo, sro, sc, image, wrow.reshape(1, F), window)
    w1, w2 = pl.pallas_call(
        other_kernel,
        out_shape=(table, table),
        in_specs=[smem] * 4 + [vmem],
        out_specs=(vmem, vmem),
        compiler_params=params,
        cost_estimate=pl.CostEstimate(flops=2**22, bytes_accessed=2 * 2**20, transcendentals=0),
        name="other_table",
    )(w_terms, fco, bo, sc, other_window)
    pieces = pl.pallas_call(
        sum_kernel,
        out_shape=[jax.ShapeDtypeStruct((256, 512), f32)] * 4,
        in_specs=[vmem] * 5,
        out_specs=[vmem] * 4,
        scratch_shapes=[pltpu.VMEM((2, 2 * F, F), bf16), pltpu.VMEM((2, F, F), bf16)],
        compiler_params=params,
        cost_estimate=pl.CostEstimate(flops=2**31, bytes_accessed=9 * 2**20, transcendentals=0),
        name="two_stages",
    )(rt, g_own, w1, w2, other_image)
    return spread(pieces)


def solution(mesh):
    torus = Mesh(mesh.devices.reshape(4, 4, 2, 4, 2), ("zh", "y", "zl", "x", "c"))
    placed = (P(None, FROW, FCOL), P(FROW), P(FCOL), P(), P(), P(), P(), P(), P())
    return jax.shard_map(local, mesh=torus, in_specs=placed, out_specs=P(None, None, FROW, FCOL), check_vma=False)
```

```python
import itertools
import math

import jax
import jax.numpy as jnp
from jax import lax
from jax.experimental import pallas as pl
from jax.experimental.pallas import tpu as pltpu
from jax.sharding import Mesh
from jax.sharding import PartitionSpec as P

IMAGE = 65536
F = 512
f32 = jnp.float32
bf16 = jnp.bfloat16
FROW = ("zh", "y")
FCOL = ("zl", "x", "c")
Z = ("zh", "zl")
PIO2 = (1.5703125, 4.837512969970703125e-4, 7.549789948768648e-8)
NT = (((1,), (1,)), ((), ()))
NN = (((1,), (0,)), ((), ()))


def sincos_of(r, q):
    z = r * r
    s = r + r * z * (-1.6666654611e-1 + z * (8.3321608736e-3 - 1.9515295891e-4 * z))
    c = 1.0 - 0.5 * z + z * z * (4.166664568298827e-2 + z * (-1.388731625493765e-3 + 2.443315711809948e-5 * z))
    odd = (q & 1) == 1
    cosine = jnp.where(odd, s, c)
    sine = jnp.where(odd, c, s)
    cosine = jnp.where(((q + 1) & 2) == 2, -cosine, cosine)
    sine = jnp.where((q & 2) == 2, -sine, sine)
    return cosine, sine


def turn(p):
    q = (p + 8192) >> 14
    r = (p - (q << 14)).astype(f32) * (2.0 * math.pi / IMAGE)
    c, s = sincos_of(r, q)
    return c, -s


def phase_index(first, second):
    high = ((first * (second >> 8)) & 255) << 8
    return (high + first * (second & 255)) & (IMAGE - 1)


def chirp(w, g):
    unit = (g & (IMAGE - 1)).astype(f32) * (1.0 / IMAGE) - 0.5
    angle = w * (unit * unit)
    n = jnp.floor(angle * (2.0 / math.pi) + 0.5)
    r = ((angle - n * PIO2[0]) - n * PIO2[1]) - n * PIO2[2]
    return sincos_of(r, n.astype(jnp.int32))


def times(a, b):
    return a[0] * b[0] - a[1] * b[1], a[0] * b[1] + a[1] * b[0]


def ids():
    return {name: lax.axis_index(name) for name in ("zh", "y", "zl", "x", "c")}


def outer(a, b):
    n = a[0].shape[1]
    big = [v[:, None, :] for v in a]
    small = [v[None, :, :] for v in b]
    return [v.reshape(-1, n) for v in times(big, small)]


def gray(i):
    return i ^ (i >> 1)


def near(own, high, low, core):
    low_first = high | (low << 1)
    high_first = low | (high << 1)
    return gray(gray(own) ^ jnp.where(core == 0, low_first, high_first))


def per_sub(sub, values):
    return jnp.where(sub == 0, values[0], values[1])


def column_factors(at, w_terms, bo, sc, offset):
    g = offset + lax.broadcasted_iota(jnp.int32, (1, F), 1)
    i = lax.broadcasted_iota(jnp.int32, (16, F), 0)
    x = near(at["x"], i >> 3, (i >> 2) & 1, at["c"])
    sub = (i >> 1) & 1
    band = per_sub(sub, [bo[sc[k]] for k in range(2)])
    coarse = turn(phase_index(g, band + (((i & 1) * 4 + x) * 2 + at["c"]) * 32))
    waves = [chirp(w_terms[sc[k]], g) for k in range(2)]
    wave = [per_sub(sub, [v[part] for v in waves]) for part in range(2)]
    fine = turn((g * lax.broadcasted_iota(jnp.int32, (32, F), 0)) & (IMAGE - 1))
    return times(coarse, wave), fine


def column_table(factors, t, table):
    coarse, fine = factors
    for zl in range(2):
        row = 2 * t + zl
        re, im = outer([v[row : row + 1] for v in coarse], fine)
        first, second = pl.ds(t * 128 + zl * 64, 32), pl.ds(t * 128 + zl * 64 + 32, 32)
        table[first, pl.ds(0, F)] = re.astype(bf16)
        table[second, pl.ds(0, F)] = im.astype(bf16)
        table[first, pl.ds(F, F)] = (-im).astype(bf16)
        table[second, pl.ds(F, F)] = re.astype(bf16)


def own_kernel(w_terms, fro, fco, bo, sro, sc, image, wrow, wcol, rt, g_out, other, table):
    at = ids()
    me = (at["zl"] * 4 + at["x"]) * 2 + at["c"]
    coarse, fine = column_factors(at, w_terms, bo, sc, fco[me])
    factors = [v * wcol[...] for v in coarse], fine
    factors_other = column_factors(at, w_terms, bo, sc, fco[me + 1 - 2 * at["c"]])
    g = fro[at["zh"] * 4 + at["y"]] + lax.broadcasted_iota(jnp.int32, (1, F), 1)
    i = lax.broadcasted_iota(jnp.int32, (16, F), 0)
    window = wrow[...] * (1.0 / 8192.0)
    fine_rows = turn((g * lax.broadcasted_iota(jnp.int32, (32, F), 0)) & (IMAGE - 1))
    y = near(at["y"], i >> 3, (i >> 2) & 1, at["c"])
    whole = jnp.concatenate([image[0], image[1]], axis=1)
    for n in range(4):
        for t in (2 * n, 2 * n + 1):
            column_table(factors, t, table)
        rows = pl.ds(n * 256, 256)
        g_out[:, rows] = lax.dot_general(whole, table[rows, :], NT, preferred_element_type=f32)
        for t in (2 * n, 2 * n + 1):
            column_table(factors_other, t, other)
        k, half = n // 2, n % 2
        if half == 0:
            wave = [v * window for v in chirp(w_terms[sc[k]], g)]
            coarse = times(turn(phase_index(g, sro[k] + ((i & 3) * 4 + y) * 32)), wave)
        re, im = outer([v[half * 8 : half * 8 + 8] for v in coarse], fine_rows)
        rt[k, pl.ds(half * 256, 256), pl.ds(0, F)] = re.astype(bf16)
        rt[k, pl.ds(half * 256, 256), pl.ds(F, F)] = im.astype(bf16)


def sum_kernel(rt, g_own, table, image, keep, to_x, to_y, to_xy, gg):
    whole = jnp.concatenate([image[0], image[1]], axis=1).astype(bf16)
    imag = (lax.broadcasted_iota(jnp.int32, (F, 128), 1) & 32) == 32
    for n in range(4):
        rows = pl.ds(n * 256, 256)
        g = g_own[:, rows] + lax.dot_general(whole, table[rows, :], NT, preferred_element_type=f32)
        for k in range(2):
            tile = g[:, k * 128 : k * 128 + 128]
            turned = jnp.where(imag, pltpu.roll(tile, 32, 1), -pltpu.roll(tile, 96, 1))
            cols = pl.ds(n * 128, 128)
            gg[k, pl.ds(0, F), cols] = tile.astype(bf16)
            gg[k, pl.ds(F, F), cols] = turned.astype(bf16)
    for k in range(2):
        for half in range(2):
            s = lax.dot_general(rt[k], gg[k, :, pl.ds(half * 256, 256)], NN, preferred_element_type=f32)
            for low in range(2):
                tile = s[:, low * 128 : low * 128 + 128]
                cols = pl.ds(low * 256 + k * 128, 128)
                (to_x if half else keep)[:, cols] = tile[:256]
                (to_xy if half else to_y)[:, cols] = tile[256:]


def swapped(value, axes, second):
    places = list(itertools.product(*map(range, (4, 4, 2, 4, 2))))
    number = {place: i for i, place in enumerate(places)}
    perm = []
    for i, (zh, y, zl, x, c) in enumerate(places):
        flip = 1 + (c ^ second)
        if "x" in axes:
            x = gray(gray(x) ^ flip)
        if "y" in axes:
            y = gray(gray(y) ^ flip)
        perm.append((i, number[zh, y, zl, x, c]))
    return lax.ppermute(value, ("zh", "y", "zl", "x", "c"), perm)


def arrived(pieces, second):
    return [pieces[0]] + [swapped(v, axes, second) for v, axes in zip(pieces[1:], ("x", "y", "xy"))]


def cut_kernel(own, by_x, by_y, by_xy, keep, to_x, to_y, to_xy):
    for y in range(2):
        for x in range(2):
            rows, cols = pl.ds(y * 128, 128), pl.ds(x * 256, 256)
            total = (own[rows, cols] + by_x[rows, cols]) + (by_y[rows, cols] + by_xy[rows, cols])
            ((keep, to_x), (to_y, to_xy))[y][x][...] = total


def pack_kernel(own, by_x, by_y, by_xy, out):
    low = lax.broadcasted_iota(jnp.int32, (128, 128), 1) < 64
    total = (own[...] + by_x[...]) + (by_y[...] + by_xy[...])
    one, two = total[:, :128], total[:, 128:]
    left = jnp.where(low, one, pltpu.roll(two, 64, 1))
    right = jnp.where(low, pltpu.roll(one, 64, 1), two)
    for zh in range(4):
        rows = slice(zh * 32, zh * 32 + 32)
        out[2 * zh] = left[rows]
        out[2 * zh + 1] = right[rows]


def last_kernel(pieces, out):
    total = jnp.sum(pieces[...], axis=0)
    for k in range(2):
        for c in range(2):
            out[k, c] = total[:, (2 * k + c) * 32 : (2 * k + c) * 32 + 32]


def spread(pieces):
    vmem = pl.BlockSpec(memory_space=pltpu.VMEM)
    params = pltpu.CompilerParams(vmem_limit_bytes=8 * 2**20)
    pieces = pl.pallas_call(
        cut_kernel,
        out_shape=[jax.ShapeDtypeStruct((128, 256), f32)] * 4,
        in_specs=[vmem] * 4,
        out_specs=[vmem] * 4,
        compiler_params=params,
        name="cut",
    )(*arrived(pieces, 0))
    packed = pl.pallas_call(
        pack_kernel,
        out_shape=jax.ShapeDtypeStruct((8, 32, 128), f32),
        in_specs=[vmem] * 4,
        out_specs=vmem,
        compiler_params=params,
        name="pack",
    )(*arrived(pieces, 1))
    blocks = lax.all_to_all(packed, ("zh", "zl"), 0, 0, tiled=True)
    return pl.pallas_call(
        last_kernel,
        out_shape=jax.ShapeDtypeStruct((2, 2, 32, 32), f32),
        in_specs=[vmem],
        out_specs=vmem,
        compiler_params=params,
        name="last_sum",
    )(blocks)


def local(image, wrow, wcol, w_terms, fro, fco, bo, sro, sc):
    smem = pl.BlockSpec(memory_space=pltpu.SMEM)
    vmem = pl.BlockSpec(memory_space=pltpu.VMEM)
    params = pltpu.CompilerParams(vmem_limit_bytes=24 * 2**20)
    swap = [(0, 1), (1, 0)]
    window = wcol.reshape(1, F)
    wide = image.astype(f32) * wcol
    other_image = lax.ppermute(wide, "c", swap)
    rt, g_own, other = pl.pallas_call(
        own_kernel,
        out_shape=(
            jax.ShapeDtypeStruct((2, F, 2 * F), bf16),
            jax.ShapeDtypeStruct((F, 2 * F), f32),
            jax.ShapeDtypeStruct((2 * F, 2 * F), bf16),
        ),
        in_specs=[smem] * 6 + [vmem] * 3,
        out_specs=(vmem, vmem, vmem),
        scratch_shapes=[pltpu.VMEM((2 * F, 2 * F), bf16)],
        compiler_params=params,
        cost_estimate=pl.CostEstimate(flops=2**31, bytes_accessed=4 * 2**20, transcendentals=0),
        name="own_facet",
    )(w_terms, fro, fco, bo, sro, sc, image, wrow.reshape(1, F), window)
    pieces = pl.pallas_call(
        sum_kernel,
        out_shape=[jax.ShapeDtypeStruct((256, 512), f32)] * 4,
        in_specs=[vmem] * 4,
        out_specs=[vmem] * 4,
        scratch_shapes=[pltpu.VMEM((2, 2 * F, F), bf16)],
        compiler_params=params,
        cost_estimate=pl.CostEstimate(flops=2**31, bytes_accessed=9 * 2**20, transcendentals=0),
        name="two_stages",
    )(rt, g_own, other, other_image)
    return spread(pieces)


def solution(mesh):
    torus = Mesh(mesh.devices.reshape(4, 4, 2, 4, 2), ("zh", "y", "zl", "x", "c"))
    placed = (P(None, FROW, FCOL), P(FROW), P(FCOL), P(), P(), P(), P(), P(), P())
    return jax.shard_map(local, mesh=torus, in_specs=placed, out_specs=P(None, None, FROW, FCOL), check_vma=False)
```

```python
import functools
import itertools
import math

import jax
import jax.numpy as jnp
from jax import lax
from jax.experimental import pallas as pl
from jax.experimental.pallas import tpu as pltpu
from jax.sharding import Mesh
from jax.sharding import PartitionSpec as P

IMAGE = 65536
F = 512
f32 = jnp.float32
bf16 = jnp.bfloat16
FROW = ("zh", "y")
FCOL = ("zl", "x", "c")
Z = ("zh", "zl")
PIO2 = (1.5703125, 4.837512969970703125e-4, 7.549789948768648e-8)
NT = (((1,), (1,)), ((), ()))
NN = (((1,), (0,)), ((), ()))


def sincos_of(r, q):
    z = r * r
    s = r + r * z * (-1.6666654611e-1 + z * (8.3321608736e-3 - 1.9515295891e-4 * z))
    c = 1.0 - 0.5 * z + z * z * (4.166664568298827e-2 + z * (-1.388731625493765e-3 + 2.443315711809948e-5 * z))
    odd = (q & 1) == 1
    cosine = jnp.where(odd, s, c)
    sine = jnp.where(odd, c, s)
    cosine = jnp.where(((q + 1) & 2) == 2, -cosine, cosine)
    sine = jnp.where((q & 2) == 2, -sine, sine)
    return cosine, sine


def turn(p):
    q = (p + 8192) >> 14
    r = (p - (q << 14)).astype(f32) * (2.0 * math.pi / IMAGE)
    c, s = sincos_of(r, q)
    return c, -s


def phase_index(first, second):
    high = ((first * (second >> 8)) & 255) << 8
    return (high + first * (second & 255)) & (IMAGE - 1)


def chirp(w, g):
    unit = (g & (IMAGE - 1)).astype(f32) * (1.0 / IMAGE) - 0.5
    angle = w * (unit * unit)
    n = jnp.floor(angle * (2.0 / math.pi) + 0.5)
    r = ((angle - n * PIO2[0]) - n * PIO2[1]) - n * PIO2[2]
    return sincos_of(r, n.astype(jnp.int32))


def times(a, b):
    return a[0] * b[0] - a[1] * b[1], a[0] * b[1] + a[1] * b[0]


def ids():
    return {name: lax.axis_index(name) for name in ("zh", "y", "zl", "x", "c")}


def outer(a, b):
    n = a[0].shape[1]
    big = [v[:, None, :] for v in a]
    small = [v[None, :, :] for v in b]
    return [v.reshape(-1, n) for v in times(big, small)]


def gray(i):
    return i ^ (i >> 1)


def near(own, high, low, core):
    low_first = high | (low << 1)
    high_first = low | (high << 1)
    return gray(gray(own) ^ jnp.where(core == 0, low_first, high_first))


def per_sub(sub, values):
    return jnp.where(sub == 0, values[0], values[1])


def column_factors(at, w_terms, bo, sc, offset):
    g = offset + lax.broadcasted_iota(jnp.int32, (1, F), 1)
    i = lax.broadcasted_iota(jnp.int32, (16, F), 0)
    x = near(at["x"], (i >> 2) & 1, (i >> 1) & 1, at["c"])
    sub = i >> 3
    band = per_sub(sub, [bo[sc[k]] for k in range(2)])
    coarse = turn(phase_index(g, band + (((i & 1) * 4 + x) * 2 + at["c"]) * 32))
    waves = [chirp(w_terms[sc[k]], g) for k in range(2)]
    wave = [per_sub(sub, [v[part] for v in waves]) for part in range(2)]
    fine = turn((g * lax.broadcasted_iota(jnp.int32, (32, F), 0)) & (IMAGE - 1))
    return times(coarse, wave), fine


def column_table(factors, t, table):
    coarse, fine = factors
    for zl in range(2):
        row = 2 * t + zl
        re, im = outer([v[row : row + 1] for v in coarse], fine)
        first, second = pl.ds(t * 128 + zl * 64, 32), pl.ds(t * 128 + zl * 64 + 32, 32)
        table[first, pl.ds(0, F)] = re.astype(bf16)
        table[second, pl.ds(0, F)] = im.astype(bf16)
        table[first, pl.ds(F, F)] = (-im).astype(bf16)
        table[second, pl.ds(F, F)] = re.astype(bf16)


def own_kernel(w_terms, fro, fco, bo, sro, sc, image, wrow, wcol, rt, g_out, other, table):
    at = ids()
    me = (at["zl"] * 4 + at["x"]) * 2 + at["c"]
    coarse, fine = column_factors(at, w_terms, bo, sc, fco[me])
    factors = [v * wcol[...] for v in coarse], fine
    factors_other = column_factors(at, w_terms, bo, sc, fco[me + 1 - 2 * at["c"]])
    g = fro[at["zh"] * 4 + at["y"]] + lax.broadcasted_iota(jnp.int32, (1, F), 1)
    i = lax.broadcasted_iota(jnp.int32, (16, F), 0)
    window = wrow[...] * (1.0 / 8192.0)
    fine_rows = turn((g * lax.broadcasted_iota(jnp.int32, (32, F), 0)) & (IMAGE - 1))
    y = near(at["y"], i >> 3, (i >> 2) & 1, at["c"])
    whole = jnp.concatenate([image[0], image[1]], axis=1)
    for n in range(4):
        for t in (2 * n, 2 * n + 1):
            column_table(factors, t, table)
        rows = pl.ds(n * 256, 256)
        g_out[:, rows] = lax.dot_general(whole, table[rows, :], NT, preferred_element_type=f32)
        for t in (2 * n, 2 * n + 1):
            column_table(factors_other, t, other)
        k, half = n // 2, n % 2
        if half == 0:
            wave = [v * window for v in chirp(w_terms[sc[k]], g)]
            coarse = times(turn(phase_index(g, sro[k] + ((i & 3) * 4 + y) * 32)), wave)
        re, im = outer([v[half * 8 : half * 8 + 8] for v in coarse], fine_rows)
        rt[k, pl.ds(half * 256, 256), pl.ds(0, F)] = re.astype(bf16)
        rt[k, pl.ds(half * 256, 256), pl.ds(F, F)] = im.astype(bf16)


def sum_kernel(k, rt, g_own, table, image, gg, to_x, to_y, to_xy):
    whole = jnp.concatenate([image[0], image[1]], axis=1).astype(bf16)
    imag = (lax.broadcasted_iota(jnp.int32, (F, 128), 1) & 32) == 32
    for n in range(2):
        rows = pl.ds(k * F + n * 256, 256)
        g = g_own[:, rows] + lax.dot_general(whole, table[rows, :], NT, preferred_element_type=f32)
        for low in range(2):
            tile = g[:, low * 128 : low * 128 + 128]
            turned = jnp.where(imag, pltpu.roll(tile, 32, 1), -pltpu.roll(tile, 96, 1))
            cols = pl.ds(n * 256 + low * 128, 128)
            gg[pl.ds(0, F), cols] = tile.astype(bf16)
            gg[pl.ds(F, F), cols] = turned.astype(bf16)
    s = lax.dot_general(rt[k], gg[:, pl.ds(256, 256)], NN, preferred_element_type=f32)
    to_x[...] = s[:256]
    to_xy[...] = s[256:]
    to_y[...] = lax.dot_general(rt[k, pl.ds(256, 256), :], gg[:, pl.ds(0, 256)], NN, preferred_element_type=f32)


def keep_kernel(rt, zero, one, keep_zero, keep_one):
    for k, (gg, keep) in enumerate(((zero, keep_zero), (one, keep_one))):
        keep[...] = lax.dot_general(rt[k, pl.ds(0, 256), :], gg[:, pl.ds(0, 256)], NN, preferred_element_type=f32)


def swapped(value, axes, second):
    places = list(itertools.product(*map(range, (4, 4, 2, 4, 2))))
    number = {place: i for i, place in enumerate(places)}
    perm = []
    for i, (zh, y, zl, x, c) in enumerate(places):
        flip = 1 + (c ^ second)
        if "x" in axes:
            x = gray(gray(x) ^ flip)
        if "y" in axes:
            y = gray(gray(y) ^ flip)
        perm.append((i, number[zh, y, zl, x, c]))
    return lax.ppermute(value, ("zh", "y", "zl", "x", "c"), perm)


def arrived(pieces, second):
    return [pieces[0]] + [swapped(v, axes, second) for v, axes in zip(pieces[1:], ("x", "y", "xy"))]


def cut_kernel(*refs):
    ins, out = refs[:8], refs[8:]
    for k in range(2):
        own, by_x, by_y, by_xy = ins[4 * k : 4 * k + 4]
        for y in range(2):
            for x in range(2):
                rows, cols = pl.ds(y * 128, 128), pl.ds(x * 128, 128)
                total = (own[rows, cols] + by_x[rows, cols]) + (by_y[rows, cols] + by_xy[rows, cols])
                out[2 * y + x][:, pl.ds(k * 128, 128)] = total


def pack_kernel(own, by_x, by_y, by_xy, out):
    low = lax.broadcasted_iota(jnp.int32, (128, 128), 1) < 64
    total = (own[...] + by_x[...]) + (by_y[...] + by_xy[...])
    one, two = total[:, :128], total[:, 128:]
    left = jnp.where(low, one, pltpu.roll(two, 64, 1))
    right = jnp.where(low, pltpu.roll(one, 64, 1), two)
    for zh in range(4):
        rows = slice(zh * 32, zh * 32 + 32)
        out[2 * zh] = left[rows]
        out[2 * zh + 1] = right[rows]


def last_kernel(pieces, out):
    total = jnp.sum(pieces[...], axis=0)
    for k in range(2):
        for c in range(2):
            out[k, c] = total[:, (2 * k + c) * 32 : (2 * k + c) * 32 + 32]


def spread(pieces):
    vmem = pl.BlockSpec(memory_space=pltpu.VMEM)
    params = pltpu.CompilerParams(vmem_limit_bytes=8 * 2**20)
    pieces = pl.pallas_call(
        cut_kernel,
        out_shape=[jax.ShapeDtypeStruct((128, 256), f32)] * 4,
        in_specs=[vmem] * 8,
        out_specs=[vmem] * 4,
        compiler_params=params,
        name="cut",
    )(*arrived(pieces[0], 0), *arrived(pieces[1], 0))
    packed = pl.pallas_call(
        pack_kernel,
        out_shape=jax.ShapeDtypeStruct((8, 32, 128), f32),
        in_specs=[vmem] * 4,
        out_specs=vmem,
        compiler_params=params,
        name="pack",
    )(*arrived(pieces, 1))
    blocks = lax.all_to_all(packed, ("zh", "zl"), 0, 0, tiled=True)
    return pl.pallas_call(
        last_kernel,
        out_shape=jax.ShapeDtypeStruct((2, 2, 32, 32), f32),
        in_specs=[vmem],
        out_specs=vmem,
        compiler_params=params,
        name="last_sum",
    )(blocks)


def local(image, wrow, wcol, w_terms, fro, fco, bo, sro, sc):
    smem = pl.BlockSpec(memory_space=pltpu.SMEM)
    vmem = pl.BlockSpec(memory_space=pltpu.VMEM)
    params = pltpu.CompilerParams(vmem_limit_bytes=24 * 2**20)
    swap = [(0, 1), (1, 0)]
    window = wcol.reshape(1, F)
    wide = image.astype(f32) * wcol
    other_image = lax.ppermute(wide, "c", swap)
    rt, g_own, other = pl.pallas_call(
        own_kernel,
        out_shape=(
            jax.ShapeDtypeStruct((2, F, 2 * F), bf16),
            jax.ShapeDtypeStruct((F, 2 * F), f32),
            jax.ShapeDtypeStruct((2 * F, 2 * F), bf16),
        ),
        in_specs=[smem] * 6 + [vmem] * 3,
        out_specs=(vmem, vmem, vmem),
        scratch_shapes=[pltpu.VMEM((2 * F, 2 * F), bf16)],
        compiler_params=params,
        cost_estimate=pl.CostEstimate(flops=2**31, bytes_accessed=4 * 2**20, transcendentals=0),
        name="own_facet",
    )(w_terms, fro, fco, bo, sro, sc, image, wrow.reshape(1, F), window)
    piece = jax.ShapeDtypeStruct((256, 256), f32)
    (zero, *sent_zero), (one, *sent_one) = [
        pl.pallas_call(
            functools.partial(sum_kernel, k),
            out_shape=[jax.ShapeDtypeStruct((2 * F, F), bf16)] + [piece] * 3,
            in_specs=[vmem] * 4,
            out_specs=[vmem] * 4,
            compiler_params=params,
            cost_estimate=pl.CostEstimate(flops=2**30, bytes_accessed=5 * 2**20, transcendentals=0),
            name=f"two_stages_{k}",
        )(rt, g_own, other, other_image)
        for k in range(2)
    ]
    keep_zero, keep_one = pl.pallas_call(
        keep_kernel,
        out_shape=[piece] * 2,
        in_specs=[vmem] * 3,
        out_specs=[vmem] * 2,
        compiler_params=params,
        cost_estimate=pl.CostEstimate(flops=2**28, bytes_accessed=3 * 2**20, transcendentals=0),
        name="keep",
    )(rt, zero, one)
    pieces = [keep_zero, *sent_zero], [keep_one, *sent_one]
    return spread(pieces)


def solution(mesh):
    torus = Mesh(mesh.devices.reshape(4, 4, 2, 4, 2), ("zh", "y", "zl", "x", "c"))
    placed = (P(None, FROW, FCOL), P(FROW), P(FCOL), P(), P(), P(), P(), P(), P())
    return jax.shard_map(local, mesh=torus, in_specs=placed, out_specs=P(None, None, FROW, FCOL), check_vma=False)
```

```python
import functools
import itertools
import math

import jax
import jax.numpy as jnp
from jax import lax
from jax.experimental import pallas as pl
from jax.experimental.pallas import tpu as pltpu
from jax.sharding import Mesh
from jax.sharding import PartitionSpec as P

IMAGE = 65536
F = 512
f32 = jnp.float32
bf16 = jnp.bfloat16
FROW = ("zh", "y")
FCOL = ("zl", "x", "c")
Z = ("zh", "zl")
PIO2 = (1.5703125, 4.837512969970703125e-4, 7.549789948768648e-8)
NT = (((1,), (1,)), ((), ()))
NN = (((1,), (0,)), ((), ()))


def sincos_of(r, q):
    z = r * r
    s = r + r * z * (-1.6666654611e-1 + z * (8.3321608736e-3 - 1.9515295891e-4 * z))
    c = 1.0 - 0.5 * z + z * z * (4.166664568298827e-2 + z * (-1.388731625493765e-3 + 2.443315711809948e-5 * z))
    odd = (q & 1) == 1
    cosine = jnp.where(odd, s, c)
    sine = jnp.where(odd, c, s)
    cosine = jnp.where(((q + 1) & 2) == 2, -cosine, cosine)
    sine = jnp.where((q & 2) == 2, -sine, sine)
    return cosine, sine


def turn(p):
    q = (p + 8192) >> 14
    r = (p - (q << 14)).astype(f32) * (2.0 * math.pi / IMAGE)
    c, s = sincos_of(r, q)
    return c, -s


def phase_index(first, second):
    high = ((first * (second >> 8)) & 255) << 8
    return (high + first * (second & 255)) & (IMAGE - 1)


def chirp(w, g):
    unit = (g & (IMAGE - 1)).astype(f32) * (1.0 / IMAGE) - 0.5
    angle = w * (unit * unit)
    n = jnp.floor(angle * (2.0 / math.pi) + 0.5)
    r = ((angle - n * PIO2[0]) - n * PIO2[1]) - n * PIO2[2]
    return sincos_of(r, n.astype(jnp.int32))


def times(a, b):
    return a[0] * b[0] - a[1] * b[1], a[0] * b[1] + a[1] * b[0]


def ids():
    return {name: lax.axis_index(name) for name in ("zh", "y", "zl", "x", "c")}


def outer(a, b):
    n = a[0].shape[1]
    big = [v[:, None, :] for v in a]
    small = [v[None, :, :] for v in b]
    return [v.reshape(-1, n) for v in times(big, small)]


def gray(i):
    return i ^ (i >> 1)


def near(own, high, low, core):
    low_first = high | (low << 1)
    high_first = low | (high << 1)
    return gray(gray(own) ^ jnp.where(core == 0, low_first, high_first))


def per_sub(sub, values):
    return jnp.where(sub == 0, values[0], values[1])


def column_factors(at, w_terms, bo, sc, offset):
    g = offset + lax.broadcasted_iota(jnp.int32, (1, F), 1)
    i = lax.broadcasted_iota(jnp.int32, (16, F), 0)
    x = near(at["x"], (i >> 2) & 1, (i >> 1) & 1, at["c"])
    sub = i >> 3
    band = per_sub(sub, [bo[sc[k]] for k in range(2)])
    coarse = turn(phase_index(g, band + (((i & 1) * 4 + x) * 2 + at["c"]) * 32))
    waves = [chirp(w_terms[sc[k]], g) for k in range(2)]
    wave = [per_sub(sub, [v[part] for v in waves]) for part in range(2)]
    fine = turn((g * lax.broadcasted_iota(jnp.int32, (32, F), 0)) & (IMAGE - 1))
    return times(coarse, wave), fine


def column_table(factors, t, table):
    coarse, fine = factors
    for zl in range(2):
        row = 2 * t + zl
        re, im = outer([v[row : row + 1] for v in coarse], fine)
        first, second = pl.ds(t * 128 + zl * 64, 32), pl.ds(t * 128 + zl * 64 + 32, 32)
        table[first, pl.ds(0, F)] = re.astype(bf16)
        table[second, pl.ds(0, F)] = im.astype(bf16)
        table[first, pl.ds(F, F)] = (-im).astype(bf16)
        table[second, pl.ds(F, F)] = re.astype(bf16)


def own_kernel(w_terms, fro, fco, bo, sro, sc, image, wrow, wcol, rt, g_out, other, table):
    at = ids()
    me = (at["zl"] * 4 + at["x"]) * 2 + at["c"]
    coarse, fine = column_factors(at, w_terms, bo, sc, fco[me])
    factors = [v * wcol[...] for v in coarse], fine
    factors_other = column_factors(at, w_terms, bo, sc, fco[me + 1 - 2 * at["c"]])
    g = fro[at["zh"] * 4 + at["y"]] + lax.broadcasted_iota(jnp.int32, (1, F), 1)
    i = lax.broadcasted_iota(jnp.int32, (16, F), 0)
    window = wrow[...] * (1.0 / 8192.0)
    fine_rows = turn((g * lax.broadcasted_iota(jnp.int32, (32, F), 0)) & (IMAGE - 1))
    y = near(at["y"], i >> 3, (i >> 2) & 1, at["c"])
    whole = jnp.concatenate([image[0], image[1]], axis=1)
    for n in range(4):
        for t in (2 * n, 2 * n + 1):
            column_table(factors, t, table)
        rows = pl.ds(n * 256, 256)
        g_out[:, rows] = lax.dot_general(whole, table[rows, :], NT, preferred_element_type=f32)
        for t in (2 * n, 2 * n + 1):
            column_table(factors_other, t, other)
        k, half = n // 2, n % 2
        if half == 0:
            wave = [v * window for v in chirp(w_terms[sc[k]], g)]
            coarse = times(turn(phase_index(g, sro[k] + ((i & 3) * 4 + y) * 32)), wave)
        re, im = outer([v[half * 8 : half * 8 + 8] for v in coarse], fine_rows)
        rt[k, pl.ds(half * 256, 256), pl.ds(0, F)] = re.astype(bf16)
        rt[k, pl.ds(half * 256, 256), pl.ds(F, F)] = im.astype(bf16)


def sum_kernel(k, rt, g_own, table, real, imaginary, gg, to_x, to_y, to_xy):
    whole = jnp.concatenate([real[...], imaginary[...]], axis=1).astype(bf16)
    imag = (lax.broadcasted_iota(jnp.int32, (F, 128), 1) & 32) == 32
    for n in range(2):
        rows = pl.ds(k * F + n * 256, 256)
        g = g_own[:, rows] + lax.dot_general(whole, table[rows, :], NT, preferred_element_type=f32)
        for low in range(2):
            tile = g[:, low * 128 : low * 128 + 128]
            turned = jnp.where(imag, pltpu.roll(tile, 32, 1), -pltpu.roll(tile, 96, 1))
            cols = pl.ds(n * 256 + low * 128, 128)
            gg[pl.ds(0, F), cols] = tile.astype(bf16)
            gg[pl.ds(F, F), cols] = turned.astype(bf16)
    s = lax.dot_general(rt[k], gg[:, pl.ds(256, 256)], NN, preferred_element_type=f32)
    to_x[...] = s[:256]
    to_xy[...] = s[256:]
    to_y[...] = lax.dot_general(rt[k, pl.ds(256, 256), :], gg[:, pl.ds(0, 256)], NN, preferred_element_type=f32)


def keep_kernel(rt, zero, one, keep_zero, keep_one):
    for k, (gg, keep) in enumerate(((zero, keep_zero), (one, keep_one))):
        keep[...] = lax.dot_general(rt[k, pl.ds(0, 256), :], gg[:, pl.ds(0, 256)], NN, preferred_element_type=f32)


def swapped(value, axes, second):
    places = list(itertools.product(*map(range, (4, 4, 2, 4, 2))))
    number = {place: i for i, place in enumerate(places)}
    perm = []
    for i, (zh, y, zl, x, c) in enumerate(places):
        flip = 1 + (c ^ second)
        if "x" in axes:
            x = gray(gray(x) ^ flip)
        if "y" in axes:
            y = gray(gray(y) ^ flip)
        perm.append((i, number[zh, y, zl, x, c]))
    return lax.ppermute(value, ("zh", "y", "zl", "x", "c"), perm)


def arrived(pieces, second):
    return [pieces[0]] + [swapped(v, axes, second) for v, axes in zip(pieces[1:], ("x", "y", "xy"))]


def cut_kernel(*refs):
    ins, out = refs[:8], refs[8:]
    for k in range(2):
        own, by_x, by_y, by_xy = ins[4 * k : 4 * k + 4]
        for y in range(2):
            for x in range(2):
                rows, cols = pl.ds(y * 128, 128), pl.ds(x * 128, 128)
                total = (own[rows, cols] + by_x[rows, cols]) + (by_y[rows, cols] + by_xy[rows, cols])
                out[2 * y + x][:, pl.ds(k * 128, 128)] = total


def pack_kernel(own, by_x, by_y, by_xy, out):
    low = lax.broadcasted_iota(jnp.int32, (128, 128), 1) < 64
    total = (own[...] + by_x[...]) + (by_y[...] + by_xy[...])
    one, two = total[:, :128], total[:, 128:]
    left = jnp.where(low, one, pltpu.roll(two, 64, 1))
    right = jnp.where(low, pltpu.roll(one, 64, 1), two)
    for zh in range(4):
        rows = slice(zh * 32, zh * 32 + 32)
        out[2 * zh] = left[rows]
        out[2 * zh + 1] = right[rows]


def last_kernel(pieces, out):
    total = jnp.sum(pieces[...], axis=0)
    for k in range(2):
        for c in range(2):
            out[k, c] = total[:, (2 * k + c) * 32 : (2 * k + c) * 32 + 32]


def spread(pieces):
    vmem = pl.BlockSpec(memory_space=pltpu.VMEM)
    params = pltpu.CompilerParams(vmem_limit_bytes=8 * 2**20)
    pieces = pl.pallas_call(
        cut_kernel,
        out_shape=[jax.ShapeDtypeStruct((128, 256), f32)] * 4,
        in_specs=[vmem] * 8,
        out_specs=[vmem] * 4,
        compiler_params=params,
        name="cut",
    )(*arrived(pieces[0], 0), *arrived(pieces[1], 0))
    packed = pl.pallas_call(
        pack_kernel,
        out_shape=jax.ShapeDtypeStruct((8, 32, 128), f32),
        in_specs=[vmem] * 4,
        out_specs=vmem,
        compiler_params=params,
        name="pack",
    )(*arrived(pieces, 1))
    blocks = lax.all_to_all(packed, ("zh", "zl"), 0, 0, tiled=True)
    return pl.pallas_call(
        last_kernel,
        out_shape=jax.ShapeDtypeStruct((2, 2, 32, 32), f32),
        in_specs=[vmem],
        out_specs=vmem,
        compiler_params=params,
        name="last_sum",
    )(blocks)


def local(image, wrow, wcol, w_terms, fro, fco, bo, sro, sc):
    smem = pl.BlockSpec(memory_space=pltpu.SMEM)
    vmem = pl.BlockSpec(memory_space=pltpu.VMEM)
    params = pltpu.CompilerParams(vmem_limit_bytes=24 * 2**20)
    swap = [(0, 1), (1, 0)]
    window = wcol.reshape(1, F)
    wide = [image[part].astype(f32) * wcol for part in range(2)]
    other_real, other_imag = [lax.ppermute(v, "c", swap) for v in wide]
    rt, g_own, other = pl.pallas_call(
        own_kernel,
        out_shape=(
            jax.ShapeDtypeStruct((2, F, 2 * F), bf16),
            jax.ShapeDtypeStruct((F, 2 * F), f32),
            jax.ShapeDtypeStruct((2 * F, 2 * F), bf16),
        ),
        in_specs=[smem] * 6 + [vmem] * 3,
        out_specs=(vmem, vmem, vmem),
        scratch_shapes=[pltpu.VMEM((2 * F, 2 * F), bf16)],
        compiler_params=params,
        cost_estimate=pl.CostEstimate(flops=2**31, bytes_accessed=4 * 2**20, transcendentals=0),
        name="own_facet",
    )(w_terms, fro, fco, bo, sro, sc, image, wrow.reshape(1, F), window)
    piece = jax.ShapeDtypeStruct((256, 256), f32)
    (zero, *sent_zero), (one, *sent_one) = [
        pl.pallas_call(
            functools.partial(sum_kernel, k),
            out_shape=[jax.ShapeDtypeStruct((2 * F, F), bf16)] + [piece] * 3,
            in_specs=[vmem] * 5,
            out_specs=[vmem] * 4,
            compiler_params=params,
            cost_estimate=pl.CostEstimate(flops=2**30, bytes_accessed=5 * 2**20, transcendentals=0),
            name=f"two_stages_{k}",
        )(rt, g_own, other, other_real, other_imag)
        for k in range(2)
    ]
    keep_zero, keep_one = pl.pallas_call(
        keep_kernel,
        out_shape=[piece] * 2,
        in_specs=[vmem] * 3,
        out_specs=[vmem] * 2,
        compiler_params=params,
        cost_estimate=pl.CostEstimate(flops=2**28, bytes_accessed=3 * 2**20, transcendentals=0),
        name="keep",
    )(rt, zero, one)
    pieces = [keep_zero, *sent_zero], [keep_one, *sent_one]
    return spread(pieces)


def solution(mesh):
    torus = Mesh(mesh.devices.reshape(4, 4, 2, 4, 2), ("zh", "y", "zl", "x", "c"))
    placed = (P(None, FROW, FCOL), P(FROW), P(FCOL), P(), P(), P(), P(), P(), P())
    return jax.shard_map(local, mesh=torus, in_specs=placed, out_specs=P(None, None, FROW, FCOL), check_vma=False)
```
